32 devices in a mesh: bx: 8 (over z, x), by: 4 (over y, core).
Axes of the slice: x: 2, y: 2, z: 4, core: 2. Of those that a mesh axis runs over, the one named last changes fastest.
Arguments:
- positions: float32 [4096, 3, 256], P(('bx', 'by')), may hold values from 0 to 4, as said below
- strengths: float32 [4096, 3, 256], P(('bx', 'by')), may hold values from -0.4 to 0.4
- blob_count: int32 [4096], P(('bx', 'by')), may hold values from 64 to 256
- split_counts: int32 [32, 32], P(('bx', 'by')), may hold values from 0 to 4, as said below
- ghost_ids: int32 [32, 8, 16], P(('bx', 'by')), may hold values from 0 to 63, as said below
- near_list: int32 [2048, 8], P(('bx', 'by')), may hold values from 0 to 191, as said below
Outputs:
- owned_blobs: float32 [2048, 6, 256], P(('bx', 'by'))
- velocity: float32 [2048, 3, 256], P(('bx', 'by'))
The draws below stay inside these ranges and needn't reach their ends.
Inputs may be any that keep to these rules, and one draw needn't show every extreme that they name: Each sender's leaves occupy its first slots, grouped by receiver in increasing order, split_counts[s, d] of them for receiver d. Every column of split_counts sums to exactly 64, and every column has an entry equal to 4. `positions`: the blobs of each used slot lie in the box of the leaf that the slot becomes; leaves are boxes of side 0.25 on a grid, and each device's leaves fill a 2 x 2 x 16 block of that grid placed by its bx and by indices. `ghost_ids`: the leaves named for a direction lie on the neighbour's face toward the reader. `near_list`: entry 0 of a leaf's list is the leaf itself; the others are leaves near it. An index 64 + q * 16 + g names ghost g of neighbour direction q and appears only where that neighbouring device exists.
All inputs are finite; a program needn't handle non-finite values.
Results may differ from the reference program's by a relative error of at most 0.0003.
Values sent between devices are 32-bit elements; how exact they have to be, the bound alone decides.
A program may use at most 64 MiB of HBM per device.

```python
import math
import jax
import jax.numpy as jnp
from jax import lax

LEAF = 256
OWN = 64
NB = 8
GP = 16
PAIR_MOST = 4
SLOTS = 128
LEAVES = 2048
N_BX = 8
N_BY = 4


OFFSET_ROWS = (-1, -1, -1, 0, 0, 1, 1, 1)


OFFSET_COLS = (-1, 0, 1, -1, 1, -1, 0, 1)


BOX_SIDE = 0.25


def split_table(key):
    devices = N_BX * N_BY
    candidate_leaves = devices * PAIR_MOST
    key_weight, key_score, key_heavy = jax.random.split(jax.random.fold_in(key, 11), 3)
    leaf_weight = jax.random.randint(key_weight, (devices,), 1, 5, dtype=jnp.int32)
    unscaled_value = jax.random.randint(key_score, (devices, candidate_leaves), 0, 8192, dtype=jnp.int32)
    sending_leaf = jnp.arange(candidate_leaves, dtype=jnp.int32) // PAIR_MOST
    heavy_leaves = jax.random.randint(key_heavy, (devices,), 0, devices, dtype=jnp.int32)
    extra_reward = jnp.where(sending_leaf[None, :] == heavy_leaves[:, None], 65536, 0).astype(jnp.int32)
    leaf_score = (unscaled_value * leaf_weight[sending_leaf][None, :] + extra_reward) * candidate_leaves + jnp.arange(candidate_leaves, dtype=jnp.int32)[None, :]
    unused, picked = lax.top_k(leaf_score, OWN)
    picked_source = picked // PAIR_MOST
    per_target = jnp.sum((picked_source[:, :, None] == jnp.arange(devices, dtype=jnp.int32)[None, None, :]).astype(jnp.int32), axis=1)
    return per_target.T


def draw_split_counts(key, part):
    return split_table(key)


def draw_positions(key, part):
    devices = N_BX * N_BY
    counts = split_table(key)
    inclusive = jnp.cumsum(counts, axis=1)
    starts = inclusive - counts
    arrive = jnp.cumsum(counts, axis=0) - counts
    slot = jnp.arange(SLOTS, dtype=jnp.int32)
    target = jnp.sum((inclusive[:, None, :] <= slot[None, :, None]).astype(jnp.int32), axis=2)
    used = target < devices
    target = jnp.minimum(target, devices - 1)
    sender = jnp.arange(devices, dtype=jnp.int32)[:, None]
    start_here = jnp.take_along_axis(starts, target, axis=1)
    arrive_here = arrive[sender, target]
    rank = jnp.where(used, arrive_here + slot[None, :] - start_here, 0)
    target_a = jnp.where(used, target // N_BY, 0)
    target_b = jnp.where(used, target % N_BY, 0)
    corner_x = (2 * target_a + rank % 2).astype(jnp.float32) * BOX_SIDE
    corner_y = (2 * target_b + rank // 2 % 2).astype(jnp.float32) * BOX_SIDE
    corner_z = (rank // 4).astype(jnp.float32) * BOX_SIDE
    corner = jnp.stack([corner_x, corner_y, corner_z], axis=2).reshape(devices * SLOTS, 3, 1)
    noise = jax.random.uniform(jax.random.fold_in(key, 23), (devices * SLOTS, 3, LEAF), jnp.float32)
    return corner + noise * BOX_SIDE


def draw_ghost_ids(key, part):
    devices = N_BX * N_BY
    key_p, key_q, key_r = jax.random.split(jax.random.fold_in(key, 31), 3)
    off_a = jnp.array(OFFSET_ROWS, jnp.int32)[None, :, None]
    off_b = jnp.array(OFFSET_COLS, jnp.int32)[None, :, None]
    free_p = jax.random.randint(key_p, (devices, 8, GP), 0, 2, dtype=jnp.int32)
    free_q = jax.random.randint(key_q, (devices, 8, GP), 0, 2, dtype=jnp.int32)
    face_p = jnp.where(off_a < 0, 1, jnp.where(off_a > 0, 0, free_p))
    face_q = jnp.where(off_b < 0, 1, jnp.where(off_b > 0, 0, free_q))
    layer = jnp.arange(GP, dtype=jnp.int32)[None, None, :] + jax.random.randint(key_r, (devices, 8, GP), -1, 2, dtype=jnp.int32)
    layer = jnp.clip(layer, 0, GP - 1)
    ids = (face_p + 2 * face_q + 4 * layer).astype(jnp.int32)
    ids = ids.at[0, 7, 0].set(0)
    ids = ids.at[0, 0, GP - 1].set(OWN - 1)
    return ids


def draw_near_list(key, part):
    rows = jnp.arange(LEAVES, dtype=jnp.int32)
    device = rows // OWN
    row_a = device // N_BY
    row_b = device % N_BY
    rank = rows % OWN
    own_p = (rank % 2)[:, None]
    own_q = (rank // 2 % 2)[:, None]
    own_r = (rank // 4)[:, None]
    key_dir, key_g, key_p, key_q, key_r = jax.random.split(jax.random.fold_in(key, 47), 5)
    shape = (LEAVES, NB)
    pick_dir = jax.random.randint(key_dir, shape, 0, 12, dtype=jnp.int32)
    direction = jnp.minimum(pick_dir, 7)
    off_a = jnp.array(OFFSET_ROWS, jnp.int32)[direction]
    off_b = jnp.array(OFFSET_COLS, jnp.int32)[direction]
    face_ok = ((off_a == 0) | (off_a == 2 * own_p - 1)) & ((off_b == 0) | (off_b == 2 * own_q - 1))
    new_a = row_a[:, None] + off_a
    new_b = row_b[:, None] + off_b
    inside = (new_a >= 0) & (new_a < N_BX) & (new_b >= 0) & (new_b < N_BY)
    use_ghost = (pick_dir < 8) & face_ok & inside
    ghost_layer = jnp.clip(own_r + jax.random.randint(key_g, shape, -1, 2, dtype=jnp.int32), 0, GP - 1)
    ghost = OWN + direction * GP + ghost_layer
    local_p = jax.random.randint(key_p, shape, 0, 2, dtype=jnp.int32)
    local_q = jax.random.randint(key_q, shape, 0, 2, dtype=jnp.int32)
    local_r = jnp.clip(own_r + jax.random.randint(key_r, shape, -1, 2, dtype=jnp.int32), 0, GP - 1)
    local = local_p + 2 * local_q + 4 * local_r
    chosen = jnp.where(use_ghost, ghost, local).astype(jnp.int32)
    chosen = chosen.at[:, 0].set(rank)
    chosen = chosen.at[OWN - 1, 1].set(OWN + 8 * GP - 1)
    return chosen


def set_ends(values, key, low, top_value):
    longest = values.shape.index(max(values.shape))
    spots = []
    for shift in (0, 1):
        where = [jax.random.randint(jax.random.fold_in(key, axis), (), 0, length) for axis, length in enumerate(values.shape)]
        where[longest] = (where[longest] + shift) % values.shape[longest]
        spots.append(tuple(where))
    return values.at[spots[0]].set(low).at[spots[1]].set(top_value)


def steps_of(rng, dims, pieces, least, largest):
    def one(axis_at, blocks):
        heights = jax.random.uniform(jax.random.fold_in(jax.random.fold_in(rng, 6), axis_at), (blocks,), jnp.float32, least / len(pieces), largest / len(pieces))
        return jnp.repeat(jnp.exp(heights), dims[axis_at] // blocks).reshape((-1,) + (1,) * (len(dims) - axis_at - 1))

    level = one(*pieces[0])
    for cut in pieces[1:]:
        level = level * one(*cut)
    return level


def centred(key, dims, scale, limit, pieces=(), kind=jnp.bfloat16):
    level = steps_of(key, dims, pieces, -0.22, 0.18) if pieces else 1.0
    values = jax.random.normal(key, dims, jnp.float32) * scale * level
    return jnp.minimum(jnp.maximum(values, -limit), limit).astype(kind)


def setup_inputs(seed: int = 0) -> dict:
    seeds = jax.random.split(jax.random.key(seed), 7)
    return {
        "positions": draw_positions(jax.random.fold_in(seeds[6], 71), 0),
        "strengths": centred(seeds[1], (N_BX * N_BY * SLOTS, 3, LEAF), 0.05, 0.4, ((0, 32),), jnp.float32),
        "blob_count": set_ends(jax.random.randint(seeds[2], (N_BX * N_BY * SLOTS,), LEAF // 4, LEAF + 1), jax.random.fold_in(seeds[2], 1), LEAF // 4, LEAF).astype(jnp.int32),
        "split_counts": draw_split_counts(jax.random.fold_in(seeds[6], 71), 0),
        "ghost_ids": draw_ghost_ids(jax.random.fold_in(seeds[6], 71), 0),
        "near_list": draw_near_list(jax.random.fold_in(seeds[6], 71), 0),
    }


CORE_SQUARED = 0.01
OFFSET_ROWS = (-1, -1, -1, 0, 0, 1, 1, 1)
OFFSET_COLS = (-1, 0, 1, -1, 1, -1, 0, 1)

def induced(targets, sources):
    delta_x = targets[:, 0, :, None] - sources[:, 0, None, :]
    delta_y = targets[:, 1, :, None] - sources[:, 1, None, :]
    delta_z = targets[:, 2, :, None] - sources[:, 2, None, :]
    inverse = lax.rsqrt(delta_x * delta_x + delta_y * delta_y + delta_z * delta_z + CORE_SQUARED)
    inverse_cube = inverse * inverse * inverse
    alpha_x = sources[:, 3, None, :]
    alpha_y = sources[:, 4, None, :]
    alpha_z = sources[:, 5, None, :]
    speed_x = lax.optimization_barrier(jnp.sum((alpha_y * delta_z - alpha_z * delta_y) * inverse_cube, axis=2))
    speed_y = lax.optimization_barrier(jnp.sum((alpha_z * delta_x - alpha_x * delta_z) * inverse_cube, axis=2))
    speed_z = lax.optimization_barrier(jnp.sum((alpha_x * delta_y - alpha_y * delta_x) * inverse_cube, axis=2))
    return jnp.stack([speed_x, speed_y, speed_z], axis=1) / (4.0 * math.pi)

def reference(positions, strengths, blob_count, split_counts, ghost_ids, near_list):
    devices = N_BX * N_BY
    starts = jnp.cumsum(split_counts, axis=1) - split_counts
    arrive = jnp.cumsum(split_counts, axis=0) - split_counts
    within = jnp.arange(PAIR_MOST, dtype=jnp.int32)
    device_ids = jnp.arange(devices, dtype=jnp.int32)
    source_slot = device_ids[:, None, None] * SLOTS + starts[:, :, None] + within[None, None, :]
    target_leaf = device_ids[None, :, None] * OWN + arrive[:, :, None] + within[None, None, :]
    valid = within[None, None, :] < split_counts[:, :, None]
    target_leaf = jnp.where(valid, target_leaf, LEAVES).astype(jnp.int32)
    anchor = jnp.zeros((LEAVES + 1,), jnp.int32).at[target_leaf.reshape(-1)].set(source_slot.reshape(-1).astype(jnp.int32))[:LEAVES]
    stacked = jnp.concatenate([positions, strengths], axis=1)[anchor]
    count = blob_count[anchor]
    live = (jnp.arange(LEAF, dtype=jnp.int32)[None, :] < count[:, None]).astype(jnp.float32)
    owned_blobs = stacked * live[:, None, :]
    rows = jnp.arange(LEAVES, dtype=jnp.int32)
    device = rows // OWN
    row_a = device // N_BY
    row_b = device % N_BY
    ghost_slot = jnp.maximum(near_list - OWN, 0)
    direction = ghost_slot // GP
    position = ghost_slot % GP
    off_a = jnp.array(OFFSET_ROWS, jnp.int32)[direction]
    off_b = jnp.array(OFFSET_COLS, jnp.int32)[direction]
    owner = (row_a[:, None] + off_a) * N_BY + row_b[:, None] + off_b
    picked = ghost_ids[device[:, None], direction, position]
    source_leaf = jnp.where(near_list < OWN, device[:, None] * OWN + near_list, owner * OWN + picked).astype(jnp.int32)

    def one_block(block_index):
        first_row = block_index * 4
        targets = lax.dynamic_slice_in_dim(owned_blobs, first_row, 4, 0)
        near_rows = lax.dynamic_slice_in_dim(source_leaf, first_row, 4, 0)
        sources = owned_blobs[near_rows]
        sources = jnp.transpose(sources, (0, 2, 1, 3)).reshape(4, 6, NB * LEAF)
        live_block = lax.dynamic_slice_in_dim(live, first_row, 4, 0)
        return induced(targets, sources) * live_block[:, None, :]
    velocity = lax.map(one_block, jnp.arange(LEAVES // 4, dtype=jnp.int32)).reshape(LEAVES, 3, LEAF)
    return (owned_blobs, velocity)
```

```python
import functools
import math

import jax
import jax.numpy as jnp
from jax import lax
from jax.experimental import pallas as pl
from jax.experimental.pallas import tpu as pltpu
from jax.sharding import PartitionSpec as P

CORE_SQUARED = 0.01
OFFSET_ROWS = (-1, -1, -1, 0, 0, 1, 1, 1)
OFFSET_COLS = (-1, 0, 1, -1, 1, -1, 0, 1)

def shifted(values, off_a, off_b, rows_bx, rows_by):
    pairs = []
    for a in range(rows_bx):
        for b in range(rows_by):
            if 0 <= a + off_a < rows_bx and 0 <= b + off_b < rows_by:
                pairs.append((a * rows_by + b, (a + off_a) * rows_by + b + off_b))
    return lax.ppermute(values, ("bx", "by"), pairs)


def split3(value):
    first = value.astype(jnp.bfloat16).astype(jnp.float32)
    rest = value - first
    second = rest.astype(jnp.bfloat16).astype(jnp.float32)
    return first, second, rest - second


def near_field(own, near, count, combined, velocity, features, moments):
    leaf = velocity.shape[2]
    near_count = near.shape[1]

    def add_corner(index, total):
        return total + combined[index, 0:3, :]

    middle = lax.fori_loop(0, own, add_corner, jnp.zeros((3, leaf), jnp.float32))[:, 0:1] / own
    ones = jnp.ones((1, leaf), jnp.float32)
    padding = jnp.zeros((8, leaf), jnp.float32)

    def prepare(index, carry):
        x = combined[index, 0:3, :] - middle
        alpha = combined[index, 3:6, :]
        a, b, c = split3(x)
        n1, n2, n3 = split3(jnp.sum(x * x, axis=0, keepdims=True))
        rows = jnp.concatenate([a, a, a, b, b, c, n1, n2, n3, ones, ones, ones, padding], axis=0)
        features[index] = rows.T.astype(jnp.bfloat16)
        moment_x = alpha[1:2] * x[2:3] - alpha[2:3] * x[1:2]
        moment_y = alpha[2:3] * x[0:1] - alpha[0:1] * x[2:3]
        moment_z = alpha[0:1] * x[1:2] - alpha[1:2] * x[0:1]
        rows = jnp.concatenate([alpha, moment_x, moment_y, moment_z, padding[0:2]], axis=0)
        high = rows.astype(jnp.bfloat16).astype(jnp.float32)
        moments[index] = jnp.concatenate([high, rows - high], axis=0).astype(jnp.bfloat16)
        return carry

    lax.fori_loop(0, combined.shape[0], prepare, 0)

    def target(index, carry):
        x = combined[index, 0:3, :] - middle
        a, b, c = split3(x)
        n1, n2, n3 = split3(jnp.sum(x * x, axis=0, keepdims=True) + CORE_SQUARED)
        rows = jnp.concatenate(
            [-2.0 * a, -2.0 * b, -2.0 * c, -2.0 * a, -2.0 * b, -2.0 * a, ones, ones, ones, n1, n2, n3, padding],
            axis=0,
        ).astype(jnp.bfloat16)
        total = jnp.zeros((16, leaf), jnp.float32)
        for entry in range(near_count):
            source = near[index, entry]
            squared = jnp.dot(features[source], rows, preferred_element_type=jnp.float32)
            inverse = lax.rsqrt(squared)
            weight = inverse * inverse * inverse
            high = weight.astype(jnp.bfloat16)
            low = (weight - high.astype(jnp.float32)).astype(jnp.bfloat16)
            left = moments[source]
            total = (
                total
                + jnp.dot(left, high, preferred_element_type=jnp.float32)
                + jnp.dot(left, low, preferred_element_type=jnp.float32)
            )
        sums = total[0:8] + total[8:16]
        speed = jnp.concatenate(
            [
                sums[1:2] * x[2:3] - sums[2:3] * x[1:2],
                sums[2:3] * x[0:1] - sums[0:1] * x[2:3],
                sums[0:1] * x[1:2] - sums[1:2] * x[0:1],
            ],
            axis=0,
        ) - sums[3:6]
        live = lax.broadcasted_iota(jnp.int32, (3, leaf), 1) < count[index]
        velocity[index] = jnp.where(live, speed * (0.25 / math.pi), 0.0)
        return carry

    lax.fori_loop(0, own, target, 0)


def local(positions, strengths, blob_count, split_counts, ghost_ids, near_list):
    rows_bx = lax.axis_size("bx")
    rows_by = lax.axis_size("by")
    devices = rows_bx * rows_by
    slots = positions.shape[0]
    pair_most = slots // devices
    leaf = positions.shape[2]
    own = near_list.shape[0]
    requests = [
        shifted(ghost_ids[0, direction], OFFSET_ROWS[direction], OFFSET_COLS[direction], rows_bx, rows_by)
        for direction in range(8)
    ]
    counts_row = split_counts[0]
    starts = jnp.cumsum(counts_row) - counts_row
    within = jnp.arange(pair_most, dtype=jnp.int32)
    pick = jnp.minimum(starts[:, None] + within[None, :], slots - 1).reshape(-1)
    valid = (within[None, :] < counts_row[:, None]).reshape(-1)
    stacked = jnp.concatenate([positions, strengths], axis=1)[pick]
    sent_count = jnp.where(valid, blob_count[pick], 0)
    sent_live = (jnp.arange(leaf, dtype=jnp.int32)[None, :] < sent_count[:, None]).astype(
        jnp.float32
    )
    outgoing = (stacked * sent_live[:, None, :]).reshape(devices, pair_most, 6, leaf)
    out_count = sent_count.astype(jnp.float32).reshape(devices, pair_most)
    arrived, arrived_count = (
        lax.all_to_all(outgoing, ("bx", "by"), split_axis=0, concat_axis=0, tiled=True),
        lax.all_to_all(out_count, ("bx", "by"), split_axis=0, concat_axis=0, tiled=True),
    )
    arrived_valid = arrived_count > 0.0
    per_source = jnp.sum(arrived_valid.astype(jnp.int32), axis=1)
    prefix = jnp.cumsum(per_source) - per_source
    placed = jnp.where(arrived_valid, prefix[:, None] + within[None, :], own).reshape(-1)
    selector = (jnp.arange(own, dtype=jnp.int32)[:, None] == placed[None, :]).astype(jnp.float32)
    owned_blobs = jnp.dot(
        selector, arrived.reshape(devices * pair_most, 6 * leaf), precision=lax.Precision.HIGHEST
    ).reshape(own, 6, leaf)
    own_count = jnp.dot(selector, arrived_count.reshape(-1), precision=lax.Precision.HIGHEST)
    ghost_blocks = []
    for direction in range(8):
        served = owned_blobs[requests[direction]]
        ghost_blocks.append(
            shifted(served, -OFFSET_ROWS[direction], -OFFSET_COLS[direction], rows_bx, rows_by)
        )
    combined = jnp.concatenate([owned_blobs] + ghost_blocks, axis=0)
    smem = pl.BlockSpec(memory_space=pltpu.SMEM)
    vmem = pl.BlockSpec(memory_space=pltpu.VMEM)
    velocity = pl.pallas_call(
        functools.partial(near_field, own),
        out_shape=jax.ShapeDtypeStruct((own, 3, leaf), jnp.float32),
        in_specs=[smem, smem, vmem],
        out_specs=vmem,
        scratch_shapes=[
            pltpu.VMEM((combined.shape[0], leaf, 32), jnp.bfloat16),
            pltpu.VMEM((combined.shape[0], 16, leaf), jnp.bfloat16),
        ],
        compiler_params=pltpu.CompilerParams(vmem_limit_bytes=48 * 1024 * 1024),
        name="near_field",
    )(near_list, own_count.astype(jnp.int32), combined)
    return (owned_blobs, velocity)


def solution(mesh):
    placed = (
        P(("bx", "by"), None, None),
        P(("bx", "by"), None, None),
        P(("bx", "by")),
        P(("bx", "by"), None),
        P(("bx", "by"), None, None),
        P(("bx", "by"), None),
    )
    return jax.shard_map(
        local,
        mesh=mesh,
        in_specs=placed,
        out_specs=(P(("bx", "by"), None, None), P(("bx", "by"), None, None)),
        check_vma=False,
    )
```

```python
import functools
import math

import jax
import jax.numpy as jnp
from jax import lax
from jax.experimental import pallas as pl
from jax.experimental.pallas import tpu as pltpu
from jax.sharding import PartitionSpec as P

CORE_SQUARED = 0.01
OFFSET_ROWS = (-1, -1, -1, 0, 0, 1, 1, 1)
OFFSET_COLS = (-1, 0, 1, -1, 1, -1, 0, 1)

def split3(value):
    first = value.astype(jnp.bfloat16).astype(jnp.float32)
    rest = value - first
    second = rest.astype(jnp.bfloat16).astype(jnp.float32)
    return first, second, rest - second


def near_field(own, near, count, combined, velocity, features, moments):
    leaf = velocity.shape[2]
    near_count = near.shape[1]

    def add_corner(index, total):
        return total + combined[index, 0:3, :]

    middle = lax.fori_loop(0, own, add_corner, jnp.zeros((3, leaf), jnp.float32))[:, 0:1] / own
    ones = jnp.ones((1, leaf), jnp.float32)
    padding = jnp.zeros((8, leaf), jnp.float32)

    def prepare(index, carry):
        x = combined[index, 0:3, :] - middle
        alpha = combined[index, 3:6, :]
        a, b, c = split3(x)
        n1, n2, n3 = split3(jnp.sum(x * x, axis=0, keepdims=True))
        rows = jnp.concatenate([a, a, a, b, b, c, n1, n2, n3, ones, ones, ones, padding], axis=0)
        features[index] = rows.T.astype(jnp.bfloat16)
        moment_x = alpha[1:2] * x[2:3] - alpha[2:3] * x[1:2]
        moment_y = alpha[2:3] * x[0:1] - alpha[0:1] * x[2:3]
        moment_z = alpha[0:1] * x[1:2] - alpha[1:2] * x[0:1]
        rows = jnp.concatenate([alpha, moment_x, moment_y, moment_z, padding[0:2]], axis=0)
        high = rows.astype(jnp.bfloat16).astype(jnp.float32)
        moments[index] = jnp.concatenate([high, rows - high], axis=0).astype(jnp.bfloat16)
        return carry

    lax.fori_loop(0, combined.shape[0], prepare, 0, unroll=4)

    def target(index, carry):
        x = combined[index, 0:3, :] - middle
        a, b, c = split3(x)
        n1, n2, n3 = split3(jnp.sum(x * x, axis=0, keepdims=True) + CORE_SQUARED)
        rows = jnp.concatenate(
            [-2.0 * a, -2.0 * b, -2.0 * c, -2.0 * a, -2.0 * b, -2.0 * a, ones, ones, ones, n1, n2, n3, padding],
            axis=0,
        ).astype(jnp.bfloat16)
        total = jnp.zeros((16, leaf), jnp.float32)
        for entry in range(near_count):
            source = near[index, entry]
            squared = jnp.dot(features[source], rows, preferred_element_type=jnp.float32)
            inverse = lax.rsqrt(squared)
            weight = inverse * inverse * inverse
            high = weight.astype(jnp.bfloat16)
            low = (weight - high.astype(jnp.float32)).astype(jnp.bfloat16)
            left = moments[source]
            total = (
                total
                + jnp.dot(left, high, preferred_element_type=jnp.float32)
                + jnp.dot(left, low, preferred_element_type=jnp.float32)
            )
        sums = total[0:8] + total[8:16]
        speed = jnp.concatenate(
            [
                sums[1:2] * x[2:3] - sums[2:3] * x[1:2],
                sums[2:3] * x[0:1] - sums[0:1] * x[2:3],
                sums[0:1] * x[1:2] - sums[1:2] * x[0:1],
            ],
            axis=0,
        ) - sums[3:6]
        live = lax.broadcasted_iota(jnp.int32, (3, leaf), 1) < count[index]
        velocity[index] = jnp.where(live, speed * (0.25 / math.pi), 0.0)
        return carry

    lax.fori_loop(0, own, target, 0)


MESH = pl.DeviceIdType.MESH


def exchange(rows_bx, rows_by, pair_most, starts, positions, strengths, arrived, outgoing, send_sem, recv_sem):
    devices = rows_bx * rows_by
    slots = positions.shape[0]
    me = lax.axis_index("bx") * rows_by + lax.axis_index("by")

    def place(step):
        other = lax.rem(me + step, devices)
        return other, (other // rows_by, lax.rem(other, rows_by))

    barrier = pltpu.get_barrier_semaphore()

    def greet(step, carry):
        pl.semaphore_signal(barrier, inc=1, device_id=place(step)[1], device_id_type=MESH)
        return carry

    lax.fori_loop(1, devices, greet, 0)

    def pack(other, target, row):
        for k in range(pair_most):
            slot = jnp.minimum(starts[other] + k, slots - 1)
            target[row, k, 0:3, :] = positions[slot]
            target[row, k, 3:6, :] = strengths[slot]

    def pack_step(step, carry):
        pack(place(step)[0], outgoing, step)
        return carry

    lax.fori_loop(1, devices, pack_step, 0)
    pack(me, arrived, me)
    pl.semaphore_wait(barrier, devices - 1)

    def copy(step):
        return pltpu.make_async_remote_copy(
            src_ref=outgoing.at[step],
            dst_ref=arrived.at[me],
            send_sem=send_sem.at[step],
            recv_sem=recv_sem.at[step],
            device_id=place(step)[1],
            device_id_type=MESH,
        )

    def start(step, carry):
        copy(step).start()
        return carry

    lax.fori_loop(1, devices, start, 0)

    def finish(step, carry):
        pltpu.make_async_remote_copy(
            src_ref=outgoing.at[step],
            dst_ref=arrived.at[lax.rem(me + devices - step, devices)],
            send_sem=send_sem.at[step],
            recv_sem=recv_sem.at[step],
            device_id=place(step)[1],
            device_id_type=MESH,
        ).wait()
        return carry

    lax.fori_loop(1, devices, finish, 0)


def ghosts(rows_bx, rows_by, own, picks, count, requests, arrived, combined, served, send_sem, recv_sem):
    leaf = arrived.shape[2]
    room = requests.shape[1]
    row_a = lax.axis_index("bx")
    row_b = lax.axis_index("by")
    barrier = pltpu.get_barrier_semaphore()

    def there(direction, sign):
        a = row_a + sign * OFFSET_ROWS[direction]
        b = row_b + sign * OFFSET_COLS[direction]
        return (a, b), (a >= 0) & (a < rows_bx) & (b >= 0) & (b < rows_by)

    for direction in range(8):
        device, exists = there(direction, 1)

        @pl.when(exists)
        def _(device=device):
            pl.semaphore_signal(barrier, inc=1, device_id=device, device_id_type=MESH)

    position = lax.broadcasted_iota(jnp.int32, (6, leaf), 1)

    def owned_leaf(index):
        return jnp.where(position < count[index], arrived[picks[index]], 0.0)

    tall = 1 + (row_a > 0).astype(jnp.int32) + (row_a < rows_bx - 1).astype(jnp.int32)
    wide = 1 + (row_b > 0).astype(jnp.int32) + (row_b < rows_by - 1).astype(jnp.int32)
    pl.semaphore_wait(barrier, tall * wide - 1)

    def copy(direction):
        return pltpu.make_async_remote_copy(
            src_ref=served.at[direction],
            dst_ref=combined.at[pl.ds(own + direction * room, room)],
            send_sem=send_sem.at[direction],
            recv_sem=recv_sem.at[direction],
            device_id=there(direction, -1)[0],
            device_id_type=MESH,
        )

    for direction in range(8):
        _, exists = there(direction, -1)

        @pl.when(exists)
        def _(direction=direction):
            def serve(index, carry):
                served[direction, index] = owned_leaf(requests[direction, index])
                return carry

            lax.fori_loop(0, room, serve, 0, unroll=4)
            copy(direction).start()

    def own_leaf(index, carry):
        combined[index] = owned_leaf(index)
        return carry

    lax.fori_loop(0, own, own_leaf, 0, unroll=4)
    for direction in range(8):
        _, exists = there(direction, -1)

        @pl.when(exists)
        def _(direction=direction):
            copy(direction).wait_send()

        _, exists = there(direction, 1)

        @pl.when(exists)
        def _(direction=direction):
            copy(direction).wait_recv()


def local(positions, strengths, blob_count, split_counts, ghost_ids, near_list):
    rows_bx = lax.axis_size("bx")
    rows_by = lax.axis_size("by")
    devices = rows_bx * rows_by
    slots = positions.shape[0]
    pair_most = slots // devices
    leaf = positions.shape[2]
    own = near_list.shape[0]
    room = ghost_ids.shape[2]
    row_a = lax.axis_index("bx")
    row_b = lax.axis_index("by")
    me = row_a * rows_by + row_b
    smem = pl.BlockSpec(memory_space=pltpu.SMEM)
    vmem = pl.BlockSpec(memory_space=pltpu.VMEM)
    counts_row = split_counts[0]
    starts = jnp.cumsum(counts_row) - counts_row
    facts = jnp.concatenate([ghost_ids.reshape(-1), counts_row, blob_count])
    table = lax.all_gather(facts, ("bx", "by"), axis=0, tiled=False)
    arrived = pl.pallas_call(
        functools.partial(exchange, rows_bx, rows_by, pair_most),
        out_shape=jax.ShapeDtypeStruct((devices, pair_most, 6, leaf), jnp.float32),
        in_specs=[smem, vmem, vmem],
        out_specs=vmem,
        scratch_shapes=[
            pltpu.VMEM((devices, pair_most, 6, leaf), jnp.float32),
            pltpu.SemaphoreType.DMA((devices,)),
            pltpu.SemaphoreType.DMA((devices,)),
        ],
        compiler_params=pltpu.CompilerParams(
            collective_id=0, has_side_effects=True, vmem_limit_bytes=32 * 1024 * 1024
        ),
        name="exchange",
    )(starts, positions, strengths)
    asked = table[:, : 8 * room].reshape(devices, 8, room)
    every = table[:, 8 * room : 8 * room + devices]
    slot_count = table[:, 8 * room + devices :]
    reader = jnp.stack(
        [me - OFFSET_ROWS[q] * rows_by - OFFSET_COLS[q] for q in range(8)]
    )
    device_ids = jnp.arange(devices, dtype=jnp.int32)
    requests = jnp.sum(
        jnp.where(device_ids[:, None, None] == reader[None, :, None], asked, 0), axis=0
    )
    to_me = jnp.sum(jnp.where(device_ids[None, :] == me, every, 0), axis=1)
    start_of = jnp.sum(jnp.where(device_ids[None, :] < me, every, 0), axis=1)
    earlier = device_ids[:, None] < device_ids[None, :]
    prefix = jnp.sum(jnp.where(earlier, to_me[:, None], 0), axis=0)
    rank = jnp.arange(own, dtype=jnp.int32)[:, None] - prefix[None, :]
    mine = (rank >= 0) & (rank < to_me[None, :])
    picks = jnp.sum(jnp.where(mine, device_ids[None, :] * pair_most + rank, 0), axis=1)
    wanted = jnp.sum(
        jnp.where(mine, device_ids[None, :] * slots + start_of[None, :] + rank, 0), axis=1
    )
    own_count = slot_count.reshape(-1)[wanted]
    combined = pl.pallas_call(
        functools.partial(ghosts, rows_bx, rows_by, own),
        out_shape=jax.ShapeDtypeStruct((own + 8 * room, 6, leaf), jnp.float32),
        in_specs=[smem, smem, smem, vmem],
        out_specs=vmem,
        scratch_shapes=[
            pltpu.VMEM((8, room, 6, leaf), jnp.float32),
            pltpu.SemaphoreType.DMA((8,)),
            pltpu.SemaphoreType.DMA((8,)),
        ],
        compiler_params=pltpu.CompilerParams(
            collective_id=1, has_side_effects=True, vmem_limit_bytes=32 * 1024 * 1024
        ),
        name="ghosts",
    )(picks, own_count, requests, arrived.reshape(devices * pair_most, 6, leaf))
    velocity = pl.pallas_call(
        functools.partial(near_field, own),
        out_shape=jax.ShapeDtypeStruct((own, 3, leaf), jnp.float32),
        in_specs=[smem, smem, vmem],
        out_specs=vmem,
        scratch_shapes=[
            pltpu.VMEM((combined.shape[0], leaf, 32), jnp.bfloat16),
            pltpu.VMEM((combined.shape[0], 16, leaf), jnp.bfloat16),
        ],
        compiler_params=pltpu.CompilerParams(vmem_limit_bytes=48 * 1024 * 1024),
        name="near_field",
    )(near_list, own_count, combined)
    return (combined[:own], velocity)


def solution(mesh):
    placed = (
        P(("bx", "by"), None, None),
        P(("bx", "by"), None, None),
        P(("bx", "by")),
        P(("bx", "by"), None),
        P(("bx", "by"), None, None),
        P(("bx", "by"), None),
    )
    return jax.shard_map(
        local,
        mesh=mesh,
        in_specs=placed,
        out_specs=(P(("bx", "by"), None, None), P(("bx", "by"), None, None)),
        check_vma=False,
    )
```

```python
import functools
import math

import jax
import jax.numpy as jnp
from jax import lax
from jax.experimental import pallas as pl
from jax.experimental.pallas import tpu as pltpu
from jax.sharding import PartitionSpec as P

CORE_SQUARED = 0.01
OFFSET_ROWS = (-1, -1, -1, 0, 0, 1, 1, 1)
OFFSET_COLS = (-1, 0, 1, -1, 1, -1, 0, 1)

def split3(value):
    first = value.astype(jnp.bfloat16).astype(jnp.float32)
    rest = value - first
    second = rest.astype(jnp.bfloat16).astype(jnp.float32)
    return first, second, rest - second


def near_field(own, near, count, combined, velocity, features, moments):
    leaf = velocity.shape[2]
    near_count = near.shape[1]

    def add_corner(index, total):
        return total + combined[index, 0:3, :]

    middle = lax.fori_loop(0, own, add_corner, jnp.zeros((3, leaf), jnp.float32))[:, 0:1] / own
    ones = jnp.ones((1, leaf), jnp.float32)
    padding = jnp.zeros((8, leaf), jnp.float32)

    def prepare(index, carry):
        x = combined[index, 0:3, :] - middle
        alpha = combined[index, 3:6, :]
        a, b, c = split3(x)
        n1, n2, n3 = split3(jnp.sum(x * x, axis=0, keepdims=True))
        rows = jnp.concatenate([a, a, a, b, b, c, n1, n2, n3, ones, ones, ones, padding], axis=0)
        features[index] = rows.T.astype(jnp.bfloat16)
        moment_x = alpha[1:2] * x[2:3] - alpha[2:3] * x[1:2]
        moment_y = alpha[2:3] * x[0:1] - alpha[0:1] * x[2:3]
        moment_z = alpha[0:1] * x[1:2] - alpha[1:2] * x[0:1]
        rows = jnp.concatenate([alpha, moment_x, moment_y, moment_z, padding[0:2]], axis=0)
        high = rows.astype(jnp.bfloat16).astype(jnp.float32)
        moments[index] = jnp.concatenate([high, rows - high], axis=0).astype(jnp.bfloat16)
        return carry

    lax.fori_loop(0, combined.shape[0], prepare, 0, unroll=4)

    def target(index, carry):
        x = combined[index, 0:3, :] - middle
        a, b, c = split3(x)
        n1, n2, n3 = split3(jnp.sum(x * x, axis=0, keepdims=True) + CORE_SQUARED)
        rows = jnp.concatenate(
            [-2.0 * a, -2.0 * b, -2.0 * c, -2.0 * a, -2.0 * b, -2.0 * a, ones, ones, ones, n1, n2, n3, padding],
            axis=0,
        ).astype(jnp.bfloat16)
        total = jnp.zeros((16, leaf), jnp.float32)
        for entry in range(near_count):
            source = near[index, entry]
            squared = jnp.dot(features[source], rows, preferred_element_type=jnp.float32)
            inverse = lax.rsqrt(squared)
            weight = inverse * inverse * inverse
            high = weight.astype(jnp.bfloat16)
            low = (weight - high.astype(jnp.float32)).astype(jnp.bfloat16)
            left = moments[source]
            total = (
                total
                + jnp.dot(left, high, preferred_element_type=jnp.float32)
                + jnp.dot(left, low, preferred_element_type=jnp.float32)
            )
        sums = total[0:8] + total[8:16]
        speed = jnp.concatenate(
            [
                sums[1:2] * x[2:3] - sums[2:3] * x[1:2],
                sums[2:3] * x[0:1] - sums[0:1] * x[2:3],
                sums[0:1] * x[1:2] - sums[1:2] * x[0:1],
            ],
            axis=0,
        ) - sums[3:6]
        live = lax.broadcasted_iota(jnp.int32, (3, leaf), 1) < count[index]
        velocity[index] = jnp.where(live, speed * (0.25 / math.pi), 0.0)
        return carry

    lax.fori_loop(0, own, target, 0)


MESH = pl.DeviceIdType.MESH


def exchange(rows_bx, rows_by, pair_most, starts, facts, positions, strengths, arrived, table, outgoing, send_sem, recv_sem, fact_send, fact_recv):
    devices = rows_bx * rows_by
    slots = positions.shape[0]
    me = lax.axis_index("bx") * rows_by + lax.axis_index("by")

    def place(step):
        other = lax.rem(me + step, devices)
        return other, (other // rows_by, lax.rem(other, rows_by))

    barrier = pltpu.get_barrier_semaphore()

    def greet(step, carry):
        pl.semaphore_signal(barrier, inc=1, device_id=place(step)[1], device_id_type=MESH)
        return carry

    lax.fori_loop(1, devices, greet, 0)

    def pack(other, target, row):
        for k in range(pair_most):
            slot = jnp.minimum(starts[other] + k, slots - 1)
            target[row, k, 0:3, :] = positions[slot]
            target[row, k, 3:6, :] = strengths[slot]

    def fact_copy(step, writer):
        return pltpu.make_async_remote_copy(
            src_ref=facts,
            dst_ref=table.at[writer],
            send_sem=fact_send.at[step],
            recv_sem=fact_recv.at[step],
            device_id=place(step)[1],
            device_id_type=MESH,
        )

    def pack_step(step, carry):
        pack(place(step)[0], outgoing, step)
        return carry

    lax.fori_loop(1, devices, pack_step, 0)
    pack(me, arrived, me)
    pl.semaphore_wait(barrier, devices - 1)

    def copy(step):
        return pltpu.make_async_remote_copy(
            src_ref=outgoing.at[step],
            dst_ref=arrived.at[me],
            send_sem=send_sem.at[step],
            recv_sem=recv_sem.at[step],
            device_id=place(step)[1],
            device_id_type=MESH,
        )

    def start(step, carry):
        fact_copy(step, me).start()
        copy(step).start()
        return carry

    lax.fori_loop(1, devices, start, 0)
    table[me] = facts[...]

    def finish(step, carry):
        pltpu.make_async_remote_copy(
            src_ref=outgoing.at[step],
            dst_ref=arrived.at[lax.rem(me + devices - step, devices)],
            send_sem=send_sem.at[step],
            recv_sem=recv_sem.at[step],
            device_id=place(step)[1],
            device_id_type=MESH,
        ).wait()
        fact_copy(step, lax.rem(me + devices - step, devices)).wait()
        return carry

    lax.fori_loop(1, devices, finish, 0)


def ghosts(rows_bx, rows_by, own, picks, count, requests, arrived, combined, served, send_sem, recv_sem):
    leaf = arrived.shape[2]
    room = requests.shape[1]
    row_a = lax.axis_index("bx")
    row_b = lax.axis_index("by")
    barrier = pltpu.get_barrier_semaphore()

    def there(direction, sign):
        a = row_a + sign * OFFSET_ROWS[direction]
        b = row_b + sign * OFFSET_COLS[direction]
        return (a, b), (a >= 0) & (a < rows_bx) & (b >= 0) & (b < rows_by)

    for direction in range(8):
        device, exists = there(direction, 1)

        @pl.when(exists)
        def _(device=device):
            pl.semaphore_signal(barrier, inc=1, device_id=device, device_id_type=MESH)

    position = lax.broadcasted_iota(jnp.int32, (6, leaf), 1)

    def owned_leaf(index):
        return jnp.where(position < count[index], arrived[picks[index]], 0.0)

    tall = 1 + (row_a > 0).astype(jnp.int32) + (row_a < rows_bx - 1).astype(jnp.int32)
    wide = 1 + (row_b > 0).astype(jnp.int32) + (row_b < rows_by - 1).astype(jnp.int32)
    pl.semaphore_wait(barrier, tall * wide - 1)

    def copy(direction):
        return pltpu.make_async_remote_copy(
            src_ref=served.at[direction],
            dst_ref=combined.at[pl.ds(own + direction * room, room)],
            send_sem=send_sem.at[direction],
            recv_sem=recv_sem.at[direction],
            device_id=there(direction, -1)[0],
            device_id_type=MESH,
        )

    for direction in range(8):
        _, exists = there(direction, -1)

        @pl.when(exists)
        def _(direction=direction):
            def serve(index, carry):
                served[direction, index] = owned_leaf(requests[direction, index])
                return carry

            lax.fori_loop(0, room, serve, 0, unroll=4)
            copy(direction).start()

    def own_leaf(index, carry):
        combined[index] = owned_leaf(index)
        return carry

    lax.fori_loop(0, own, own_leaf, 0, unroll=4)
    for direction in range(8):
        _, exists = there(direction, -1)

        @pl.when(exists)
        def _(direction=direction):
            copy(direction).wait_send()

        _, exists = there(direction, 1)

        @pl.when(exists)
        def _(direction=direction):
            copy(direction).wait_recv()


def local(positions, strengths, blob_count, split_counts, ghost_ids, near_list):
    rows_bx = lax.axis_size("bx")
    rows_by = lax.axis_size("by")
    devices = rows_bx * rows_by
    slots = positions.shape[0]
    pair_most = slots // devices
    leaf = positions.shape[2]
    own = near_list.shape[0]
    room = ghost_ids.shape[2]
    row_a = lax.axis_index("bx")
    row_b = lax.axis_index("by")
    me = row_a * rows_by + row_b
    smem = pl.BlockSpec(memory_space=pltpu.SMEM)
    vmem = pl.BlockSpec(memory_space=pltpu.VMEM)
    counts_row = split_counts[0]
    starts = jnp.cumsum(counts_row) - counts_row
    facts = jnp.concatenate([ghost_ids.reshape(-1), counts_row, blob_count])
    lines = -(-facts.shape[0] // 128)
    facts = jnp.pad(facts, (0, lines * 128 - facts.shape[0])).reshape(lines, 128)
    arrived, table = pl.pallas_call(
        functools.partial(exchange, rows_bx, rows_by, pair_most),
        out_shape=(
            jax.ShapeDtypeStruct((devices, pair_most, 6, leaf), jnp.float32),
            jax.ShapeDtypeStruct((devices, lines, 128), jnp.int32),
        ),
        in_specs=[smem, vmem, vmem, vmem],
        out_specs=(vmem, vmem),
        scratch_shapes=[
            pltpu.VMEM((devices, pair_most, 6, leaf), jnp.float32),
            pltpu.SemaphoreType.DMA((devices,)),
            pltpu.SemaphoreType.DMA((devices,)),
            pltpu.SemaphoreType.DMA((devices,)),
            pltpu.SemaphoreType.DMA((devices,)),
        ],
        compiler_params=pltpu.CompilerParams(
            collective_id=0, has_side_effects=True, vmem_limit_bytes=32 * 1024 * 1024
        ),
        name="exchange",
    )(starts, facts, positions, strengths)
    table = table.reshape(devices, lines * 128)
    asked = table[:, : 8 * room].reshape(devices, 8, room)
    every = table[:, 8 * room : 8 * room + devices]
    slot_count = table[:, 8 * room + devices : 8 * room + devices + slots]
    reader = jnp.stack(
        [me - OFFSET_ROWS[q] * rows_by - OFFSET_COLS[q] for q in range(8)]
    )
    device_ids = jnp.arange(devices, dtype=jnp.int32)
    requests = jnp.sum(
        jnp.where(device_ids[:, None, None] == reader[None, :, None], asked, 0), axis=0
    )
    to_me = jnp.sum(jnp.where(device_ids[None, :] == me, every, 0), axis=1)
    start_of = jnp.sum(jnp.where(device_ids[None, :] < me, every, 0), axis=1)
    earlier = device_ids[:, None] < device_ids[None, :]
    prefix = jnp.sum(jnp.where(earlier, to_me[:, None], 0), axis=0)
    rank = jnp.arange(own, dtype=jnp.int32)[:, None] - prefix[None, :]
    mine = (rank >= 0) & (rank < to_me[None, :])
    picks = jnp.sum(jnp.where(mine, device_ids[None, :] * pair_most + rank, 0), axis=1)
    wanted = jnp.sum(
        jnp.where(mine, device_ids[None, :] * slots + start_of[None, :] + rank, 0), axis=1
    )
    own_count = slot_count.reshape(-1)[wanted]
    combined = pl.pallas_call(
        functools.partial(ghosts, rows_bx, rows_by, own),
        out_shape=jax.ShapeDtypeStruct((own + 8 * room, 6, leaf), jnp.float32),
        in_specs=[smem, smem, smem, vmem],
        out_specs=vmem,
        scratch_shapes=[
            pltpu.VMEM((8, room, 6, leaf), jnp.float32),
            pltpu.SemaphoreType.DMA((8,)),
            pltpu.SemaphoreType.DMA((8,)),
        ],
        compiler_params=pltpu.CompilerParams(
            collective_id=1, has_side_effects=True, vmem_limit_bytes=32 * 1024 * 1024
        ),
        name="ghosts",
    )(picks, own_count, requests, arrived.reshape(devices * pair_most, 6, leaf))
    velocity = pl.pallas_call(
        functools.partial(near_field, own),
        out_shape=jax.ShapeDtypeStruct((own, 3, leaf), jnp.float32),
        in_specs=[smem, smem, vmem],
        out_specs=vmem,
        scratch_shapes=[
            pltpu.VMEM((combined.shape[0], leaf, 32), jnp.bfloat16),
            pltpu.VMEM((combined.shape[0], 16, leaf), jnp.bfloat16),
        ],
        compiler_params=pltpu.CompilerParams(vmem_limit_bytes=48 * 1024 * 1024),
        name="near_field",
    )(near_list, own_count, combined)
    return (combined[:own], velocity)


def solution(mesh):
    placed = (
        P(("bx", "by"), None, None),
        P(("bx", "by"), None, None),
        P(("bx", "by")),
        P(("bx", "by"), None),
        P(("bx", "by"), None, None),
        P(("bx", "by"), None),
    )
    return jax.shard_map(
        local,
        mesh=mesh,
        in_specs=placed,
        out_specs=(P(("bx", "by"), None, None), P(("bx", "by"), None, None)),
        check_vma=False,
    )
```

```python
import functools
import math

import jax
import jax.numpy as jnp
from jax import lax
from jax.experimental import pallas as pl
from jax.experimental.pallas import tpu as pltpu
from jax.sharding import PartitionSpec as P

CORE_SQUARED = 0.01
OFFSET_ROWS = (-1, -1, -1, 0, 0, 1, 1, 1)
OFFSET_COLS = (-1, 0, 1, -1, 1, -1, 0, 1)

def split3(value):
    first = value.astype(jnp.bfloat16).astype(jnp.float32)
    rest = value - first
    second = rest.astype(jnp.bfloat16).astype(jnp.float32)
    return first, second, rest - second


def near_field(own, near, count, combined, velocity, features, moments):
    leaf = velocity.shape[2]
    near_count = near.shape[1]

    def add_corner(index, total):
        return total + combined[index, 0:3, :]

    middle = lax.fori_loop(0, own, add_corner, jnp.zeros((3, leaf), jnp.float32))[:, 0:1] / own
    ones = jnp.ones((1, leaf), jnp.float32)
    padding = jnp.zeros((8, leaf), jnp.float32)

    def prepare(index, carry):
        x = combined[index, 0:3, :] - middle
        alpha = combined[index, 3:6, :]
        a, b, c = split3(x)
        n1, n2, n3 = split3(jnp.sum(x * x, axis=0, keepdims=True))
        rows = jnp.concatenate([a, a, a, b, b, c, n1, n2, n3, ones, ones, ones, padding], axis=0)
        features[index] = rows.T.astype(jnp.bfloat16)
        moment_x = alpha[1:2] * x[2:3] - alpha[2:3] * x[1:2]
        moment_y = alpha[2:3] * x[0:1] - alpha[0:1] * x[2:3]
        moment_z = alpha[0:1] * x[1:2] - alpha[1:2] * x[0:1]
        rows = jnp.concatenate([alpha, moment_x, moment_y, moment_z, padding[0:2]], axis=0)
        high = rows.astype(jnp.bfloat16).astype(jnp.float32)
        moments[index] = jnp.concatenate([high, rows - high], axis=0).astype(jnp.bfloat16)
        return carry

    lax.fori_loop(0, combined.shape[0], prepare, 0, unroll=4)

    def target(index, carry):
        x = combined[index, 0:3, :] - middle
        a, b, c = split3(x)
        n1, n2, n3 = split3(jnp.sum(x * x, axis=0, keepdims=True) + CORE_SQUARED)
        rows = jnp.concatenate(
            [-2.0 * a, -2.0 * b, -2.0 * c, -2.0 * a, -2.0 * b, -2.0 * a, ones, ones, ones, n1, n2, n3, padding],
            axis=0,
        ).astype(jnp.bfloat16)
        total = jnp.zeros((16, leaf), jnp.float32)
        for entry in range(near_count):
            source = near[index, entry]
            squared = jnp.dot(features[source], rows, preferred_element_type=jnp.float32)
            inverse = lax.rsqrt(squared)
            weight = inverse * inverse * inverse
            high = weight.astype(jnp.bfloat16)
            low = (weight - high.astype(jnp.float32)).astype(jnp.bfloat16)
            left = moments[source]
            total = (
                total
                + jnp.dot(left, high, preferred_element_type=jnp.float32)
                + jnp.dot(left, low, preferred_element_type=jnp.float32)
            )
        sums = total[0:8] + total[8:16]
        speed = jnp.concatenate(
            [
                sums[1:2] * x[2:3] - sums[2:3] * x[1:2],
                sums[2:3] * x[0:1] - sums[0:1] * x[2:3],
                sums[0:1] * x[1:2] - sums[1:2] * x[0:1],
            ],
            axis=0,
        ) - sums[3:6]
        live = lax.broadcasted_iota(jnp.int32, (3, leaf), 1) < count[index]
        velocity[index] = jnp.where(live, speed * (0.25 / math.pi), 0.0)
        return carry

    lax.fori_loop(0, own, target, 0, unroll=8)


MESH = pl.DeviceIdType.MESH


def exchange(rows_bx, rows_by, pair_most, starts, facts, positions, strengths, arrived, table, outgoing, send_sem, recv_sem, fact_send, fact_recv):
    devices = rows_bx * rows_by
    slots = positions.shape[0]
    me = lax.axis_index("bx") * rows_by + lax.axis_index("by")

    def place(step):
        other = lax.rem(me + step, devices)
        return other, (other // rows_by, lax.rem(other, rows_by))

    barrier = pltpu.get_barrier_semaphore()

    def greet(step, carry):
        pl.semaphore_signal(barrier, inc=1, device_id=place(step)[1], device_id_type=MESH)
        return carry

    lax.fori_loop(1, devices, greet, 0)

    def pack(other, target, row):
        for k in range(pair_most):
            slot = jnp.minimum(starts[other] + k, slots - 1)
            target[row, k, 0:3, :] = positions[slot]
            target[row, k, 3:6, :] = strengths[slot]

    def fact_copy(step, writer):
        return pltpu.make_async_remote_copy(
            src_ref=facts,
            dst_ref=table.at[writer],
            send_sem=fact_send.at[step],
            recv_sem=fact_recv.at[step],
            device_id=place(step)[1],
            device_id_type=MESH,
        )

    def pack_step(step, carry):
        pack(place(step)[0], outgoing, step)
        return carry

    lax.fori_loop(1, devices, pack_step, 0)
    pack(me, arrived, me)
    pl.semaphore_wait(barrier, devices - 1)

    def copy(step):
        return pltpu.make_async_remote_copy(
            src_ref=outgoing.at[step],
            dst_ref=arrived.at[me],
            send_sem=send_sem.at[step],
            recv_sem=recv_sem.at[step],
            device_id=place(step)[1],
            device_id_type=MESH,
        )

    def start(step, carry):
        fact_copy(step, me).start()
        copy(step).start()
        return carry

    lax.fori_loop(1, devices, start, 0)
    table[me] = facts[...]

    def finish(step, carry):
        pltpu.make_async_remote_copy(
            src_ref=outgoing.at[step],
            dst_ref=arrived.at[lax.rem(me + devices - step, devices)],
            send_sem=send_sem.at[step],
            recv_sem=recv_sem.at[step],
            device_id=place(step)[1],
            device_id_type=MESH,
        ).wait()
        fact_copy(step, lax.rem(me + devices - step, devices)).wait()
        return carry

    lax.fori_loop(1, devices, finish, 0)


def ghosts(rows_bx, rows_by, own, picks, count, requests, arrived, combined, served, send_sem, recv_sem):
    leaf = arrived.shape[2]
    room = requests.shape[1]
    row_a = lax.axis_index("bx")
    row_b = lax.axis_index("by")
    barrier = pltpu.get_barrier_semaphore()

    def there(direction, sign):
        a = row_a + sign * OFFSET_ROWS[direction]
        b = row_b + sign * OFFSET_COLS[direction]
        return (a, b), (a >= 0) & (a < rows_bx) & (b >= 0) & (b < rows_by)

    for direction in range(8):
        device, exists = there(direction, 1)

        @pl.when(exists)
        def _(device=device):
            pl.semaphore_signal(barrier, inc=1, device_id=device, device_id_type=MESH)

    position = lax.broadcasted_iota(jnp.int32, (6, leaf), 1)

    def owned_leaf(index):
        return jnp.where(position < count[index], arrived[picks[index]], 0.0)

    tall = 1 + (row_a > 0).astype(jnp.int32) + (row_a < rows_bx - 1).astype(jnp.int32)
    wide = 1 + (row_b > 0).astype(jnp.int32) + (row_b < rows_by - 1).astype(jnp.int32)
    pl.semaphore_wait(barrier, tall * wide - 1)

    def copy(direction):
        return pltpu.make_async_remote_copy(
            src_ref=served.at[direction],
            dst_ref=combined.at[pl.ds(own + direction * room, room)],
            send_sem=send_sem.at[direction],
            recv_sem=recv_sem.at[direction],
            device_id=there(direction, -1)[0],
            device_id_type=MESH,
        )

    for direction in range(8):
        _, exists = there(direction, -1)

        @pl.when(exists)
        def _(direction=direction):
            def serve(index, carry):
                served[direction, index] = owned_leaf(requests[direction, index])
                return carry

            lax.fori_loop(0, room, serve, 0, unroll=4)
            copy(direction).start()

    def own_leaf(index, carry):
        combined[index] = owned_leaf(index)
        return carry

    lax.fori_loop(0, own, own_leaf, 0, unroll=4)
    for direction in range(8):
        _, exists = there(direction, -1)

        @pl.when(exists)
        def _(direction=direction):
            copy(direction).wait_send()

        _, exists = there(direction, 1)

        @pl.when(exists)
        def _(direction=direction):
            copy(direction).wait_recv()


def local(positions, strengths, blob_count, split_counts, ghost_ids, near_list):
    rows_bx = lax.axis_size("bx")
    rows_by = lax.axis_size("by")
    devices = rows_bx * rows_by
    slots = positions.shape[0]
    pair_most = slots // devices
    leaf = positions.shape[2]
    own = near_list.shape[0]
    room = ghost_ids.shape[2]
    row_a = lax.axis_index("bx")
    row_b = lax.axis_index("by")
    me = row_a * rows_by + row_b
    smem = pl.BlockSpec(memory_space=pltpu.SMEM)
    vmem = pl.BlockSpec(memory_space=pltpu.VMEM)
    counts_row = split_counts[0]
    starts = jnp.cumsum(counts_row) - counts_row
    facts = jnp.concatenate([ghost_ids.reshape(-1), counts_row, blob_count])
    lines = -(-facts.shape[0] // 128)
    facts = jnp.pad(facts, (0, lines * 128 - facts.shape[0])).reshape(lines, 128)
    arrived, table = pl.pallas_call(
        functools.partial(exchange, rows_bx, rows_by, pair_most),
        out_shape=(
            jax.ShapeDtypeStruct((devices, pair_most, 6, leaf), jnp.float32),
            jax.ShapeDtypeStruct((devices, lines, 128), jnp.int32),
        ),
        in_specs=[smem, vmem, vmem, vmem],
        out_specs=(vmem, vmem),
        scratch_shapes=[
            pltpu.VMEM((devices, pair_most, 6, leaf), jnp.float32),
            pltpu.SemaphoreType.DMA((devices,)),
            pltpu.SemaphoreType.DMA((devices,)),
            pltpu.SemaphoreType.DMA((devices,)),
            pltpu.SemaphoreType.DMA((devices,)),
        ],
        compiler_params=pltpu.CompilerParams(
            collective_id=0, has_side_effects=True, vmem_limit_bytes=32 * 1024 * 1024
        ),
        name="exchange",
    )(starts, facts, positions, strengths)
    table = table.reshape(devices, lines * 128)
    asked = table[:, : 8 * room].reshape(devices, 8, room)
    every = table[:, 8 * room : 8 * room + devices]
    slot_count = table[:, 8 * room + devices : 8 * room + devices + slots]
    reader = jnp.stack(
        [me - OFFSET_ROWS[q] * rows_by - OFFSET_COLS[q] for q in range(8)]
    )
    device_ids = jnp.arange(devices, dtype=jnp.int32)
    requests = jnp.sum(
        jnp.where(device_ids[:, None, None] == reader[None, :, None], asked, 0), axis=0
    )
    to_me = jnp.sum(jnp.where(device_ids[None, :] == me, every, 0), axis=1)
    start_of = jnp.sum(jnp.where(device_ids[None, :] < me, every, 0), axis=1)
    earlier = device_ids[:, None] < device_ids[None, :]
    prefix = jnp.sum(jnp.where(earlier, to_me[:, None], 0), axis=0)
    rank = jnp.arange(own, dtype=jnp.int32)[:, None] - prefix[None, :]
    mine = (rank >= 0) & (rank < to_me[None, :])
    picks = jnp.sum(jnp.where(mine, device_ids[None, :] * pair_most + rank, 0), axis=1)
    wanted = jnp.sum(
        jnp.where(mine, device_ids[None, :] * slots + start_of[None, :] + rank, 0), axis=1
    )
    own_count = slot_count.reshape(-1)[wanted]
    combined = pl.pallas_call(
        functools.partial(ghosts, rows_bx, rows_by, own),
        out_shape=jax.ShapeDtypeStruct((own + 8 * room, 6, leaf), jnp.float32),
        in_specs=[smem, smem, smem, vmem],
        out_specs=vmem,
        scratch_shapes=[
            pltpu.VMEM((8, room, 6, leaf), jnp.float32),
            pltpu.SemaphoreType.DMA((8,)),
            pltpu.SemaphoreType.DMA((8,)),
        ],
        compiler_params=pltpu.CompilerParams(
            collective_id=1, has_side_effects=True, vmem_limit_bytes=32 * 1024 * 1024
        ),
        name="ghosts",
    )(picks, own_count, requests, arrived.reshape(devices * pair_most, 6, leaf))
    velocity = pl.pallas_call(
        functools.partial(near_field, own),
        out_shape=jax.ShapeDtypeStruct((own, 3, leaf), jnp.float32),
        in_specs=[smem, smem, vmem],
        out_specs=vmem,
        scratch_shapes=[
            pltpu.VMEM((combined.shape[0], leaf, 32), jnp.bfloat16),
            pltpu.VMEM((combined.shape[0], 16, leaf), jnp.bfloat16),
        ],
        compiler_params=pltpu.CompilerParams(vmem_limit_bytes=48 * 1024 * 1024),
        name="near_field",
    )(near_list, own_count, combined)
    return (combined[:own], velocity)


def solution(mesh):
    placed = (
        P(("bx", "by"), None, None),
        P(("bx", "by"), None, None),
        P(("bx", "by")),
        P(("bx", "by"), None),
        P(("bx", "by"), None, None),
        P(("bx", "by"), None),
    )
    return jax.shard_map(
        local,
        mesh=mesh,
        in_specs=placed,
        out_specs=(P(("bx", "by"), None, None), P(("bx", "by"), None, None)),
        check_vma=False,
    )
```

```python
import functools
import math

import jax
import jax.numpy as jnp
from jax import lax
from jax.experimental import pallas as pl
from jax.experimental.pallas import tpu as pltpu
from jax.sharding import PartitionSpec as P

CORE_SQUARED = 0.01
OFFSET_ROWS = (-1, -1, -1, 0, 0, 1, 1, 1)
OFFSET_COLS = (-1, 0, 1, -1, 1, -1, 0, 1)

def split3(value):
    first = value.astype(jnp.bfloat16).astype(jnp.float32)
    rest = value - first
    second = rest.astype(jnp.bfloat16).astype(jnp.float32)
    return first, second, rest - second


def near_field(own, near, count, combined, velocity, features, moments):
    leaf = velocity.shape[2]
    near_count = near.shape[1]

    def add_corner(index, total):
        return total + combined[index, 0:3, :]

    middle = lax.fori_loop(0, own, add_corner, jnp.zeros((3, leaf), jnp.float32))[:, 0:1] / own
    ones = jnp.ones((1, leaf), jnp.float32)
    padding = jnp.zeros((8, leaf), jnp.float32)

    def prepare(index, carry):
        x = combined[index, 0:3, :] - middle
        alpha = combined[index, 3:6, :]
        a, b, c = split3(x)
        n1, n2, n3 = split3(jnp.sum(x * x, axis=0, keepdims=True))
        rows = jnp.concatenate([a, a, a, b, b, c, n1, n2, n3, ones, ones, ones, padding], axis=0)
        features[index] = rows.T.astype(jnp.bfloat16)
        moment_x = alpha[1:2] * x[2:3] - alpha[2:3] * x[1:2]
        moment_y = alpha[2:3] * x[0:1] - alpha[0:1] * x[2:3]
        moment_z = alpha[0:1] * x[1:2] - alpha[1:2] * x[0:1]
        rows = jnp.concatenate([alpha, moment_x, moment_y, moment_z, padding[0:2]], axis=0)
        high = rows.astype(jnp.bfloat16).astype(jnp.float32)
        moments[index] = jnp.concatenate([high, rows - high], axis=0).astype(jnp.bfloat16)
        return carry

    lax.fori_loop(0, combined.shape[0], prepare, 0, unroll=4)

    def target(index, carry):
        x = combined[index, 0:3, :] - middle
        a, b, c = split3(x)
        n1, n2, n3 = split3(jnp.sum(x * x, axis=0, keepdims=True) + CORE_SQUARED)
        rows = jnp.concatenate(
            [-2.0 * a, -2.0 * b, -2.0 * c, -2.0 * a, -2.0 * b, -2.0 * a, ones, ones, ones, n1, n2, n3, padding],
            axis=0,
        ).astype(jnp.bfloat16)
        total = jnp.zeros((16, leaf), jnp.float32)
        for entry in range(near_count):
            source = near[index, entry]
            squared = jnp.dot(features[source], rows, preferred_element_type=jnp.float32)
            inverse = lax.rsqrt(squared)
            weight = inverse * inverse * inverse
            high = weight.astype(jnp.bfloat16)
            low = (weight - high.astype(jnp.float32)).astype(jnp.bfloat16)
            left = moments[source]
            total = (
                total
                + jnp.dot(left, high, preferred_element_type=jnp.float32)
                + jnp.dot(left, low, preferred_element_type=jnp.float32)
            )
        sums = total[0:8] + total[8:16]
        speed = jnp.concatenate(
            [
                sums[1:2] * x[2:3] - sums[2:3] * x[1:2],
                sums[2:3] * x[0:1] - sums[0:1] * x[2:3],
                sums[0:1] * x[1:2] - sums[1:2] * x[0:1],
            ],
            axis=0,
        ) - sums[3:6]
        live = lax.broadcasted_iota(jnp.int32, (3, leaf), 1) < count[index]
        velocity[index] = jnp.where(live, speed * (0.25 / math.pi), 0.0)
        return carry

    lax.fori_loop(0, own, target, 0, unroll=8)


MESH = pl.DeviceIdType.MESH


def exchange(rows_bx, rows_by, pair_most, starts, facts, positions, strengths, arrived, table, outgoing, send_sem, recv_sem, fact_send, fact_recv):
    devices = rows_bx * rows_by
    slots = positions.shape[0]
    me = lax.axis_index("bx") * rows_by + lax.axis_index("by")

    def place(step):
        other = lax.rem(me + step, devices)
        return other, (other // rows_by, lax.rem(other, rows_by))

    barrier = pltpu.get_barrier_semaphore()

    def greet(step, carry):
        pl.semaphore_signal(barrier, inc=1, device_id=place(step)[1], device_id_type=MESH)
        return carry

    lax.fori_loop(1, devices, greet, 0)

    def pack(other, target, row):
        for k in range(pair_most):
            slot = jnp.minimum(starts[other] + k, slots - 1)
            target[row, k, 0:3, :] = positions[slot]
            target[row, k, 3:6, :] = strengths[slot]

    def fact_copy(step, writer):
        return pltpu.make_async_remote_copy(
            src_ref=facts,
            dst_ref=table.at[writer],
            send_sem=fact_send.at[step],
            recv_sem=fact_recv.at[step],
            device_id=place(step)[1],
            device_id_type=MESH,
        )

    pl.semaphore_wait(barrier, devices - 1)

    def copy(step):
        return pltpu.make_async_remote_copy(
            src_ref=outgoing.at[step],
            dst_ref=arrived.at[me],
            send_sem=send_sem.at[step],
            recv_sem=recv_sem.at[step],
            device_id=place(step)[1],
            device_id_type=MESH,
        )

    def start(step, carry):
        pack(place(step)[0], outgoing, step)
        copy(step).start()
        fact_copy(step, me).start()
        return carry

    lax.fori_loop(1, devices, start, 0)
    table[me] = facts[...]
    pack(me, arrived, me)

    def finish(step, carry):
        pltpu.make_async_remote_copy(
            src_ref=outgoing.at[step],
            dst_ref=arrived.at[lax.rem(me + devices - step, devices)],
            send_sem=send_sem.at[step],
            recv_sem=recv_sem.at[step],
            device_id=place(step)[1],
            device_id_type=MESH,
        ).wait()
        fact_copy(step, lax.rem(me + devices - step, devices)).wait()
        return carry

    lax.fori_loop(1, devices, finish, 0)


def ghosts(rows_bx, rows_by, own, picks, count, requests, arrived, combined, served, send_sem, recv_sem):
    leaf = arrived.shape[2]
    room = requests.shape[1]
    row_a = lax.axis_index("bx")
    row_b = lax.axis_index("by")
    barrier = pltpu.get_barrier_semaphore()

    def there(direction, sign):
        a = row_a + sign * OFFSET_ROWS[direction]
        b = row_b + sign * OFFSET_COLS[direction]
        return (a, b), (a >= 0) & (a < rows_bx) & (b >= 0) & (b < rows_by)

    for direction in range(8):
        device, exists = there(direction, 1)

        @pl.when(exists)
        def _(device=device):
            pl.semaphore_signal(barrier, inc=1, device_id=device, device_id_type=MESH)

    position = lax.broadcasted_iota(jnp.int32, (6, leaf), 1)

    def owned_leaf(index):
        return jnp.where(position < count[index], arrived[picks[index]], 0.0)

    tall = 1 + (row_a > 0).astype(jnp.int32) + (row_a < rows_bx - 1).astype(jnp.int32)
    wide = 1 + (row_b > 0).astype(jnp.int32) + (row_b < rows_by - 1).astype(jnp.int32)
    pl.semaphore_wait(barrier, tall * wide - 1)

    def copy(direction):
        return pltpu.make_async_remote_copy(
            src_ref=served.at[direction],
            dst_ref=combined.at[pl.ds(own + direction * room, room)],
            send_sem=send_sem.at[direction],
            recv_sem=recv_sem.at[direction],
            device_id=there(direction, -1)[0],
            device_id_type=MESH,
        )

    for direction in range(8):
        _, exists = there(direction, -1)

        @pl.when(exists)
        def _(direction=direction):
            def serve(index, carry):
                served[direction, index] = owned_leaf(requests[direction, index])
                return carry

            lax.fori_loop(0, room, serve, 0, unroll=4)
            copy(direction).start()

    def own_leaf(index, carry):
        combined[index] = owned_leaf(index)
        return carry

    lax.fori_loop(0, own, own_leaf, 0, unroll=4)
    for direction in range(8):
        _, exists = there(direction, -1)

        @pl.when(exists)
        def _(direction=direction):
            copy(direction).wait_send()

        _, exists = there(direction, 1)

        @pl.when(exists)
        def _(direction=direction):
            copy(direction).wait_recv()


def local(positions, strengths, blob_count, split_counts, ghost_ids, near_list):
    rows_bx = lax.axis_size("bx")
    rows_by = lax.axis_size("by")
    devices = rows_bx * rows_by
    slots = positions.shape[0]
    pair_most = slots // devices
    leaf = positions.shape[2]
    own = near_list.shape[0]
    room = ghost_ids.shape[2]
    row_a = lax.axis_index("bx")
    row_b = lax.axis_index("by")
    me = row_a * rows_by + row_b
    smem = pl.BlockSpec(memory_space=pltpu.SMEM)
    vmem = pl.BlockSpec(memory_space=pltpu.VMEM)
    counts_row = split_counts[0]
    starts = jnp.cumsum(counts_row) - counts_row
    facts = jnp.concatenate([ghost_ids.reshape(-1), counts_row, blob_count])
    lines = -(-facts.shape[0] // 128)
    facts = jnp.pad(facts, (0, lines * 128 - facts.shape[0])).reshape(lines, 128)
    arrived, table = pl.pallas_call(
        functools.partial(exchange, rows_bx, rows_by, pair_most),
        out_shape=(
            jax.ShapeDtypeStruct((devices, pair_most, 6, leaf), jnp.float32),
            jax.ShapeDtypeStruct((devices, lines, 128), jnp.int32),
        ),
        in_specs=[smem, vmem, vmem, vmem],
        out_specs=(vmem, vmem),
        scratch_shapes=[
            pltpu.VMEM((devices, pair_most, 6, leaf), jnp.float32),
            pltpu.SemaphoreType.DMA((devices,)),
            pltpu.SemaphoreType.DMA((devices,)),
            pltpu.SemaphoreType.DMA((devices,)),
            pltpu.SemaphoreType.DMA((devices,)),
        ],
        compiler_params=pltpu.CompilerParams(
            collective_id=0, has_side_effects=True, vmem_limit_bytes=32 * 1024 * 1024
        ),
        name="exchange",
    )(starts, facts, positions, strengths)
    table = table.reshape(devices, lines * 128)
    asked = table[:, : 8 * room].reshape(devices, 8, room)
    every = table[:, 8 * room : 8 * room + devices]
    slot_count = table[:, 8 * room + devices : 8 * room + devices + slots]
    reader = jnp.stack(
        [me - OFFSET_ROWS[q] * rows_by - OFFSET_COLS[q] for q in range(8)]
    )
    device_ids = jnp.arange(devices, dtype=jnp.int32)
    requests = jnp.sum(
        jnp.where(device_ids[:, None, None] == reader[None, :, None], asked, 0), axis=0
    )
    to_me = jnp.sum(jnp.where(device_ids[None, :] == me, every, 0), axis=1)
    start_of = jnp.sum(jnp.where(device_ids[None, :] < me, every, 0), axis=1)
    earlier = device_ids[:, None] < device_ids[None, :]
    prefix = jnp.sum(jnp.where(earlier, to_me[:, None], 0), axis=0)
    rank = jnp.arange(own, dtype=jnp.int32)[:, None] - prefix[None, :]
    mine = (rank >= 0) & (rank < to_me[None, :])
    picks = jnp.sum(jnp.where(mine, device_ids[None, :] * pair_most + rank, 0), axis=1)
    wanted = jnp.sum(
        jnp.where(mine, device_ids[None, :] * slots + start_of[None, :] + rank, 0), axis=1
    )
    own_count = slot_count.reshape(-1)[wanted]
    combined = pl.pallas_call(
        functools.partial(ghosts, rows_bx, rows_by, own),
        out_shape=jax.ShapeDtypeStruct((own + 8 * room, 6, leaf), jnp.float32),
        in_specs=[smem, smem, smem, vmem],
        out_specs=vmem,
        scratch_shapes=[
            pltpu.VMEM((8, room, 6, leaf), jnp.float32),
            pltpu.SemaphoreType.DMA((8,)),
            pltpu.SemaphoreType.DMA((8,)),
        ],
        compiler_params=pltpu.CompilerParams(
            collective_id=1, has_side_effects=True, vmem_limit_bytes=32 * 1024 * 1024
        ),
        name="ghosts",
    )(picks, own_count, requests, arrived.reshape(devices * pair_most, 6, leaf))
    velocity = pl.pallas_call(
        functools.partial(near_field, own),
        out_shape=jax.ShapeDtypeStruct((own, 3, leaf), jnp.float32),
        in_specs=[smem, smem, vmem],
        out_specs=vmem,
        scratch_shapes=[
            pltpu.VMEM((combined.shape[0], leaf, 32), jnp.bfloat16),
            pltpu.VMEM((combined.shape[0], 16, leaf), jnp.bfloat16),
        ],
        compiler_params=pltpu.CompilerParams(vmem_limit_bytes=48 * 1024 * 1024),
        name="near_field",
    )(near_list, own_count, combined)
    return (combined[:own], velocity)


def solution(mesh):
    placed = (
        P(("bx", "by"), None, None),
        P(("bx", "by"), None, None),
        P(("bx", "by")),
        P(("bx", "by"), None),
        P(("bx", "by"), None, None),
        P(("bx", "by"), None),
    )
    return jax.shard_map(
        local,
        mesh=mesh,
        in_specs=placed,
        out_specs=(P(("bx", "by"), None, None), P(("bx", "by"), None, None)),
        check_vma=False,
    )
```
